128 devices in a mesh: dp: 32 (over y, z, core), tensor: 4 (over x).
Axes of the slice: x: 4, y: 4, z: 4, core: 2. Of those that a mesh axis runs over, the one named last changes fastest.
Arguments:
- inputs: bfloat16 [16384, 4096], P(('dp', 'tensor')), may hold values from -60 to 60
- output_gradient: bfloat16 [16384, 4096], P('dp', 'tensor'), may hold values from -60 to 60
- frozen: bfloat16 [4096, 4096], P('tensor'), may hold values from -0.09375 to 0.09375
- adapter_down_weight: bfloat16 [16, 4096], replicated, may hold values from -0.09375 to 0.09375
- adapter_up_weight: bfloat16 [16, 4096], P(None, 'tensor'), may hold values from -0.09375 to 0.09375
Outputs:
- input_gradient: bfloat16 [16384, 4096], P(('dp', 'tensor'))
- act_factor: float32 [4096, 4096], P('dp', 'tensor')
- grad_factor: float32 [4096, 4096], P('dp', 'tensor')
- grad_down: float32 [16, 4096], P(None, 'tensor')
- up_gradient_mean: float32 [16, 4096], P(None, 'tensor')
The draws below stay inside these ranges and needn't reach their ends.
All inputs are finite; a program needn't handle non-finite values.
Results may differ from the reference program's by a relative error of at most 0.014.
Values may be sent and summed in bfloat16 or wider, within the bound.
No kernel may reach another device: no remote copies, remote signals or barrier semaphores. Data moves between devices by JAX's collectives and lax.ppermute only.
A program may use at most 256 MiB of HBM per device.

```python
import jax
import jax.numpy as jnp

INPUT_FEATURES = 4096
QUERY_FEATURES = 4096
ADAPTER_RANK = 16
TOKEN_COUNT = 16384


def rough_field(keys, rows, cols, base):
    row_scale = jnp.exp(jax.random.uniform(keys[0], (rows, 1), jnp.float32, -1.15, 1.15))
    col_scale = jnp.exp(jax.random.uniform(keys[1], (1, cols), jnp.float32, -1.15, 1.15))
    return base * row_scale * col_scale


def draw_inputs(key, part):
    key = jax.random.fold_in(key, 11)
    keys = jax.random.split(key, 4)
    base = jnp.clip(jax.random.normal(keys[2], (TOKEN_COUNT, INPUT_FEATURES), jnp.float32), -5.5, 5.5)
    return rough_field(keys, TOKEN_COUNT, INPUT_FEATURES, base).astype(jnp.bfloat16)


def draw_output_gradient(key, part):
    key = jax.random.fold_in(key, 12)
    keys = jax.random.split(key, 4)
    base = jnp.clip(jax.random.normal(keys[2], (TOKEN_COUNT, QUERY_FEATURES), jnp.float32), -5.5, 5.5)
    return rough_field(keys, TOKEN_COUNT, QUERY_FEATURES, base).astype(jnp.bfloat16)


def block_scale(key, shape, pieces, least, high):
    def one(axis_at, shards_of):
        heights = jax.random.uniform(jax.random.fold_in(jax.random.fold_in(key, 6), axis_at), (shards_of,), jnp.float32, least / len(pieces), high / len(pieces))
        return jnp.repeat(jnp.exp(heights), shape[axis_at] // shards_of).reshape((-1,) + (1,) * (len(shape) - axis_at - 1))

    gain = one(*pieces[0])
    for cut in pieces[1:]:
        gain = gain * one(*cut)
    return gain


def noise(own_key, shape, spread, reach, pieces=(), kind=jnp.bfloat16):
    drawn = jax.random.normal(own_key, shape, jnp.float32) * spread
    if len(pieces) > 0:
        drawn = block_scale(own_key, shape, pieces, -0.22, 0.18) * drawn
    return jnp.clip(drawn, min=-reach, max=reach).astype(kind)


def setup_inputs(seed: int = 0) -> dict:
    key_of = jax.random.split(jax.random.key(seed), 6)
    inputs = draw_inputs(jax.random.fold_in(key_of[5], 71), 0)
    output_gradient = draw_output_gradient(jax.random.fold_in(key_of[5], 71), 0)
    frozen = noise(key_of[2], (QUERY_FEATURES, INPUT_FEATURES), QUERY_FEATURES ** -0.5, 0.09375, ((0, 4),))
    adapter_down_weight = noise(key_of[3], (ADAPTER_RANK, INPUT_FEATURES), INPUT_FEATURES ** -0.5, 0.09375)
    adapter_up_weight = noise(key_of[4], (ADAPTER_RANK, QUERY_FEATURES), QUERY_FEATURES ** -0.5, 0.09375, ((1, 4),))
    return {"inputs": inputs, "output_gradient": output_gradient, "frozen": frozen, "adapter_down_weight": adapter_down_weight, "adapter_up_weight": adapter_up_weight}


adapter_scale = 2.0


def reference(inputs, output_gradient, frozen, adapter_down_weight, adapter_up_weight):
    rank_activation = jnp.dot(inputs, adapter_down_weight.T, preferred_element_type=jnp.float32).astype(jnp.bfloat16)
    adapter_update = (adapter_scale * jnp.dot(output_gradient, adapter_up_weight.T, preferred_element_type=jnp.float32)).astype(jnp.bfloat16)
    input_gradient = (jnp.dot(output_gradient, frozen, preferred_element_type=jnp.float32)
                  + jnp.dot(adapter_update, adapter_down_weight, preferred_element_type=jnp.float32)).astype(jnp.bfloat16)
    act_factor = jnp.dot(inputs.T, inputs, preferred_element_type=jnp.float32) / TOKEN_COUNT
    grad_factor = jnp.dot(output_gradient.T, output_gradient, preferred_element_type=jnp.float32) / TOKEN_COUNT
    grad_down = jnp.dot(adapter_update.T, inputs, preferred_element_type=jnp.float32) / TOKEN_COUNT
    up_gradient_mean = adapter_scale * jnp.dot(rank_activation.T, output_gradient, preferred_element_type=jnp.float32) / TOKEN_COUNT
    return input_gradient, act_factor, grad_factor, grad_down, up_gradient_mean
```

```python
import jax
import jax.numpy as jnp
from jax import lax
from jax.sharding import Mesh, PartitionSpec as P

adapter_scale = 2.0
f32 = jnp.float32
bf16 = jnp.bfloat16
ring = 4


def shift(array, axis, step):
    size = lax.axis_size(axis)
    return lax.ppermute(array, axis, [(i, (i + step) % size) for i in range(size)])


def cols(array, start, width):
    return lax.dynamic_slice_in_dim(array, start, width, 1)


def rows(array, start, width):
    return lax.dynamic_slice_in_dim(array, start, width, 0)


def outer(left, right):
    return lax.dot_general(left, right, (((0,), (0,)), ((), ())), preferred_element_type=f32)


def nt(left, right):
    return lax.dot_general(left, right, (((1,), (1,)), ((), ())), preferred_element_type=f32)


def mm(left, right):
    return jnp.dot(left, right, preferred_element_type=f32)


def ring_scatter(two, plus, minus, axis):
    half = two.shape[1] // 2
    from_left = shift(two[:, :half], axis, 1)
    from_right = shift(two[:, half:], axis, -1)
    plus = jnp.concatenate(
        [(plus[:, :half].astype(f32) + from_left.astype(f32)).astype(bf16), plus[:, half:]], 1
    )
    minus = jnp.concatenate(
        [minus[:, :half], (minus[:, half:].astype(f32) + from_right.astype(f32)).astype(bf16)], 1
    )
    return shift(plus, axis, 1), shift(minus, axis, -1)


def ring_sum(value, axis):
    one, three, two = shift(value, axis, 1), shift(value, axis, -1), shift(value, axis, 2)
    return (value + two) + (one + three)


def per_device(inputs, output_gradient, frozen, down, up):
    x, y, z, c = (lax.axis_index(name) for name in "xyzc")
    total = inputs.shape[0] * 128
    tok, width = output_gradient.shape
    own_rows = tok // ring
    sub = width // 8

    def core_bit(array, bit):
        return jnp.concatenate([cols(array, (2 * i + bit) * sub, sub) for i in range(ring)], 1)

    first = core_bit(output_gradient, c)
    sibling_gradient = shift(output_gradient, "c", 1)
    first_left, first_right = shift(first, "x", 1), shift(first, "x", -1)
    x_left, x_right = shift(inputs, "y", 1), shift(inputs, "y", -1)
    second = core_bit(sibling_gradient, c)
    second_left, second_right = shift(second, "x", 1), shift(second, "x", -1)
    first_far, second_far = shift(first_left, "x", 1), shift(second_right, "x", -1)
    half = inputs.shape[0] // 2
    far_low, far_high = shift(x_left[:half], "y", 1), shift(x_right[half:], "y", -1)
    mine = [inputs, x_left, x_right, far_low, far_high]
    tokens = jnp.concatenate(mine + [shift(piece, "c", 1) for piece in mine], 0)

    low = nt(down, inputs).astype(bf16)
    delta_part = nt(up, output_gradient)
    relative = [rows(output_gradient, (x + k) % ring * own_rows, own_rows) for k in range(ring)]
    packs = [
        jnp.concatenate([low.astype(f32), cols(delta_part, (x + k) % ring * own_rows, own_rows)], 0)
        for k in range(ring)
    ]
    got = [packs[0]] + [shift(packs[(-k) % ring], "x", (-k) % ring) for k in range(1, ring)]
    rank = down.shape[0]
    delta = (
        adapter_scale * ((got[0][rank:] + got[1][rank:]) + (got[2][rank:] + got[3][rank:]))
    ).astype(bf16)
    low_all = jnp.concatenate([piece[:rank] for piece in got], 1).astype(bf16)
    rolled = jnp.concatenate(relative, 0)
    up_part = adapter_scale * mm(low_all, rolled)
    down_part = mm(delta, inputs)
    down_pieces = [cols(down_part, (x + k) % ring * width, width) for k in range(ring)]
    down_sum = (down_pieces[0] + shift(down_pieces[2], "x", 2)) + (
        shift(down_pieces[1], "x", 1) + shift(down_pieces[3], "x", 3)
    )
    small = jnp.concatenate([down_sum, up_part], 0)
    small = ring_sum(ring_sum(small, "z"), "y")
    small = (small + shift(small, "c", 1)) / total

    part = [mm(relative[k], frozen).astype(bf16) for k in (2, 1, 3)]
    right, left = ring_scatter(*part, "x")
    input_gradient = (
        (mm(relative[0], frozen) + lax.dot_general(delta, down, (((0,), (0,)), ((), ())), preferred_element_type=f32))
        + (left.astype(f32) + right.astype(f32))
    ).astype(bf16)

    own_left = jnp.stack([first, first_right, first_far, first_left])
    own_both = jnp.stack([second, second_right, second_far, second_left])

    def gradient_piece(k):
        at = (y + k - x) % ring
        a = lax.dynamic_index_in_dim(own_left, at, 0, False)
        b = lax.dynamic_index_in_dim(own_both, at, 0, False)
        return outer(a, output_gradient) + outer(b, sibling_gradient)

    part = [gradient_piece(k).astype(bf16) for k in (2, 1, 3)]
    right, left = ring_scatter(*part, "y")
    reduced = gradient_piece(0) + (left.astype(f32) + right.astype(f32))
    pieces = [rows(reduced, (z + k) % ring * sub, sub) for k in range(ring)]
    far, plus, minus = (shift(pieces[k].astype(bf16), "z", k).astype(f32) for k in (2, 1, 3))
    grad_factor = (pieces[0] + far + (plus + minus)) / total

    def activation_piece(k):
        return outer(cols(tokens, y * width + (z + k) % ring * (2 * sub) + c * sub, sub), tokens)

    part = [activation_piece(k).astype(bf16) for k in (2, 1, 3)]
    right, left = ring_scatter(*part, "z")
    reduced = activation_piece(0) + (left.astype(f32) + right.astype(f32))
    pieces = [cols(reduced, (x + k) % ring * width, width) for k in range(ring)]
    far, plus, minus = (shift(pieces[k].astype(bf16), "x", k).astype(f32) for k in (2, 1, 3))
    act_factor = (pieces[0] + far + (plus + minus)) / total
    return input_gradient, act_factor, grad_factor, small[:rank], small[rank:]


def solution(mesh):
    fine = Mesh(mesh.devices.reshape(ring, ring, 2, ring), ("y", "z", "c", "x"))
    dp = ("y", "z", "c")
    return jax.shard_map(
        per_device,
        mesh=fine,
        in_specs=(P(dp + ("x",), None), P(dp, "x"), P("x", None), P(), P(None, "x")),
        out_specs=(P(dp + ("x",), None), P(dp, "x"), P(dp, "x"), P(None, "x"), P(None, "x")),
        check_vma=False,
    )
```

```python
import functools

import jax
import jax.numpy as jnp
from jax import lax
from jax.experimental import pallas as pl
from jax.experimental.pallas import tpu as pltpu
from jax.sharding import Mesh, PartitionSpec as P

adapter_scale = 2.0
f32 = jnp.float32
bf16 = jnp.bfloat16
ring = 4
lane = 128
vmem = 60 * 2**20
hbm = pl.BlockSpec(memory_space=pltpu.MemorySpace.HBM)
light = pl.CostEstimate(flops=2**10, bytes_accessed=2**10, transcendentals=0)


def shift(array, axis, step):
    size = lax.axis_size(axis)
    return lax.ppermute(array, axis, [(i, (i + step) % size) for i in range(size)])


def exchange(array, axis, step):
    return lax.ppermute(array, axis, [(i, i ^ step) for i in range(lax.axis_size(axis))])


def travel(array, axis, step):
    size = lax.axis_size(axis)
    sign = (1, -1)
    order = ("c", axis) if axis == "x" else (axis, "c")
    place = (lambda i, c: size * c + i) if axis == "x" else (lambda i, c: 2 * i + c)
    pairs = [(place(i, c), place((i + step * sign[c]) % size, c)) for i in range(size) for c in range(2)]
    return lax.ppermute(array, order, pairs)


def together(*values):
    return lax.optimization_barrier(values)


def cols(array, start, width):
    return lax.dynamic_slice_in_dim(array, start, width, 1)


def rows(array, start, width):
    return lax.dynamic_slice_in_dim(array, start, width, 0)


def nt(left, right):
    return lax.dot_general(left, right, (((1,), (1,)), ((), ())), preferred_element_type=f32)


def tn(left, right):
    return lax.dot_general(left, right, (((0,), (0,)), ((), ())), preferred_element_type=f32)


def mm(left, right):
    return jnp.dot(left, right, preferred_element_type=f32)


def run_all(copies):
    for copy in copies:
        copy.start()
    for copy in copies:
        copy.wait()


def share_kernel(left, right, out):
    out[...] = mm(left[...], right[...]).astype(bf16)


def share_product(left, right, tile=512):
    return pl.pallas_call(
        share_kernel,
        grid=(right.shape[1] // tile,),
        in_specs=[
            pl.BlockSpec(left.shape, lambda j: (0, 0)),
            pl.BlockSpec((right.shape[0], tile), lambda j: (0, j)),
        ],
        out_specs=pl.BlockSpec((left.shape[0], tile), lambda j: (0, j)),
        out_shape=jax.ShapeDtypeStruct((left.shape[0], right.shape[1]), bf16),
        compiler_params=pltpu.CompilerParams(vmem_limit_bytes=vmem),
        cost_estimate=pl.CostEstimate(
            flops=2 * left.size * right.shape[1], bytes_accessed=2 * right.size, transcendentals=0
        ),
    )(left, right)


def small_kernel(place, *refs):
    messages, inputs, down, up = refs[:ring], refs[ring], refs[ring + 1], refs[ring + 2]
    held, weights, sems = refs[ring + 3 :]
    tok = inputs.shape[0]
    width = held.shape[2]
    rank = weights.shape[1]
    copies = []
    for k, ref in enumerate(messages):
        own = pl.ds(pl.multiple_of(place[0] * tok, tok), tok)
        copies.append(pltpu.make_async_copy(ref.at[own], held.at[k], sems.at[0, k]))
        copies.append(pltpu.make_async_copy(ref.at[pl.ds(ring * tok, rank)], weights.at[k], sems.at[1, k]))
    run_all(copies)
    both = [nt(weights[k], held[k]) for k in range(ring)]
    delta = (adapter_scale * ((both[0] + both[2]) + (both[1] + both[3]))).astype(bf16)
    up[...] = delta
    down[...] = mm(delta, inputs[...])


def small_terms(messages, inputs, place):
    tok, width = inputs.shape
    rank = 16
    return pl.pallas_call(
        small_kernel,
        grid_spec=pltpu.PrefetchScalarGridSpec(
            num_scalar_prefetch=1,
            grid=(1,),
            in_specs=[hbm] * ring + [pl.BlockSpec((tok, width), lambda j, o: (0, 0))],
            out_specs=[
                pl.BlockSpec((rank, width), lambda j, o: (0, 0)),
                pl.BlockSpec((rank, tok), lambda j, o: (0, 0)),
            ],
            scratch_shapes=[
                pltpu.VMEM((ring, tok, messages[0].shape[1]), bf16),
                pltpu.VMEM((ring, rank, messages[0].shape[1]), bf16),
                pltpu.SemaphoreType.DMA((2, ring)),
            ],
        ),
        out_shape=[jax.ShapeDtypeStruct((rank, width), f32), jax.ShapeDtypeStruct((rank, tok), bf16)],
        compiler_params=pltpu.CompilerParams(vmem_limit_bytes=vmem),
        cost_estimate=light,
    )(place, *messages, inputs)


def stack(pairs, held, sems):
    copies = []
    at = 0
    for n, (ref, size) in enumerate(pairs):
        copies.append(pltpu.make_async_copy(ref.at[pl.ds(0, size)], held.at[pl.ds(at, size)], sems.at[n]))
        copies[-1].start()
        at += size
    return copies


def turn(held, offsets, turned):
    for i in range(ring):
        start = pl.multiple_of(offsets[i], lane)
        turned[i * lane : (i + 1) * lane] = held[:, pl.ds(start, lane)].T


def gradient_kernel(numbers, *refs):
    own, sibling, outs = refs[:ring], refs[ring : 2 * ring], refs[2 * ring : 3 * ring]
    held, low, turned, staged, sems, low_sems, out_sems = refs[3 * ring :]
    tok, width = held.shape[1] // 2, held.shape[2]
    sub = ring * lane
    rank = low.shape[0]
    arrivals = [stack(((own[j], tok), (sibling[j], tok)), held.at[j], sems.at[j]) for j in range(ring)]
    more = []
    for half, refs_of in enumerate((own, sibling)):
        for j in range(ring):
            start = pl.multiple_of(half * tok + numbers[2 * ring + j], lane)
            more.append(
                pltpu.make_async_copy(
                    refs_of[j].at[pl.ds(tok + rank, rank), pl.ds(0, lane)],
                    low.at[:, pl.ds(start, lane)],
                    low_sems.at[half, j],
                )
            )
            more[-1].start()
    for j in range(ring):
        for copy in arrivals[j]:
            copy.wait()
        turn(held.at[j], numbers, turned)
        for i in range(2):
            part = slice(i * width // 2, (i + 1) * width // 2)
            staged[numbers[ring + j], :sub, part] = mm(turned[...], held[0, :, part]).astype(bf16)
    for copy in more:
        copy.wait()
    extra = mm(low[...], held[0]).astype(bf16)
    for k in range(ring):
        staged[k, sub:] = extra
    run_all([pltpu.make_async_copy(staged.at[k], outs[k], out_sems.at[k]) for k in range(ring)])


def gradient_pieces(own, sibling, numbers, tok):
    width = own[0].shape[1]
    sub = ring * lane
    rank = (own[0].shape[0] - tok) // 2
    return pl.pallas_call(
        gradient_kernel,
        grid_spec=pltpu.PrefetchScalarGridSpec(
            num_scalar_prefetch=1,
            grid=(1,),
            in_specs=[hbm] * (2 * ring),
            out_specs=[hbm] * ring,
            scratch_shapes=[
                pltpu.VMEM((ring, 2 * tok, width), bf16),
                pltpu.VMEM((rank, 2 * tok), bf16),
                pltpu.VMEM((sub, 2 * tok), bf16),
                pltpu.VMEM((ring, sub + rank, width), bf16),
                pltpu.SemaphoreType.DMA((ring, 2)),
                pltpu.SemaphoreType.DMA((2, ring)),
                pltpu.SemaphoreType.DMA((ring,)),
            ],
        ),
        out_shape=[jax.ShapeDtypeStruct((sub + rank, width), bf16)] * ring,
        compiler_params=pltpu.CompilerParams(vmem_limit_bytes=vmem),
        cost_estimate=light,
    )(numbers, *own, *sibling)


def activation_kernel(tile, numbers, *refs):
    count = len(refs) - ring - 8
    pieces, extra, outs = refs[:count], refs[count : count + 2], refs[count + 2 : count + 2 + ring]
    held, turned, staged, more, sems, out_sems = refs[count + 2 + ring :]
    width = held.shape[1]
    arrivals = stack([(ref, ref.shape[0]) for ref in pieces], held, sems)
    rest = [pltpu.make_async_copy(ref, more.at[i], sems.at[count + i]) for i, ref in enumerate(extra)]
    for copy in rest:
        copy.start()
    for copy in arrivals:
        copy.wait()
    turn(held, numbers, turned)
    for copy in rest:
        copy.wait()
    term = (more[0] + more[1]).astype(bf16)
    for k in range(ring):
        staged[k, lane:] = term
    sent = []
    for j in range(width // tile):
        part = slice(j * tile, (j + 1) * tile)
        result = mm(turned[...], held[:, part]).astype(bf16)
        for k in range(ring):
            staged[k, :lane, part] = result[k * lane : (k + 1) * lane]
            sent.append(pltpu.make_async_copy(staged.at[k, :, part], outs[k].at[:, part], out_sems.at[j, k]))
            sent[-1].start()
    for copy in sent:
        copy.wait()


def activation_pieces(pieces, extra, numbers, tile=512):
    count, width = len(pieces), pieces[0].shape[1]
    tokens = sum(piece.shape[0] for piece in pieces)
    rank = extra[0].shape[0]
    return pl.pallas_call(
        functools.partial(activation_kernel, tile),
        grid_spec=pltpu.PrefetchScalarGridSpec(
            num_scalar_prefetch=1,
            grid=(1,),
            in_specs=[hbm] * (count + 2),
            out_specs=[hbm] * ring,
            scratch_shapes=[
                pltpu.VMEM((tokens, width), bf16),
                pltpu.VMEM((ring * lane, tokens), bf16),
                pltpu.VMEM((ring, lane + rank, width), bf16),
                pltpu.VMEM((2, rank, width), f32),
                pltpu.SemaphoreType.DMA((count + 2,)),
                pltpu.SemaphoreType.DMA((width // tile, ring)),
            ],
        ),
        out_shape=[jax.ShapeDtypeStruct((lane + rank, width), bf16)] * ring,
        compiler_params=pltpu.CompilerParams(vmem_limit_bytes=vmem),
        cost_estimate=light,
    )(numbers, *pieces, *extra)


def per_device(inputs, output_gradient, frozen, down, up):
    x, y, z, c = (lax.axis_index(name) for name in "xyzc")
    total = inputs.shape[0] * 128
    tok, width = output_gradient.shape
    own_rows = tok // ring
    rank = down.shape[0]
    steps = jnp.arange(ring, dtype=jnp.int32)
    ahead = jnp.where(c == 0, steps, -steps)
    row_offsets = y * width + (z + ahead) % ring * (2 * lane) + c * lane
    slots = (jnp.where(c == 0, x - y, y - x) + steps) % ring
    numbers = jnp.concatenate([(2 * steps + c) * lane, slots, (x + ahead) % ring * lane])

    x_behind, x_ahead = travel(inputs, "y", 1), travel(inputs, "y", -1)
    low = jnp.pad(nt(down, inputs).astype(bf16), ((0, 0), (0, width - inputs.shape[0])))
    message = jnp.concatenate([output_gradient, up, low], 0)
    message_behind, message_ahead = travel(message, "x", 1), travel(message, "x", -1)
    sibling_message, sibling_inputs = shift(message, "c", 1), shift(inputs, "c", 1)
    share = share_product(output_gradient, frozen).reshape(ring, own_rows, -1)
    message_behind, message_ahead, x_behind, x_ahead, sibling_message, sibling_inputs, numbers, row_offsets = together(
        message_behind, message_ahead, x_behind, x_ahead, sibling_message, sibling_inputs, numbers, row_offsets
    )
    message_far = travel(message_behind, "x", 1)
    x_far = travel(x_behind, "y", 1)
    message_far, x_far, share = together(message_far, x_far, share)
    messages = [message, message_ahead, message_far, message_behind]
    sibling_messages = [sibling_message] + [shift(messages[-k], "c", 1) for k in range(1, ring)]
    tokens = [inputs, x_ahead, x_behind, x_far]
    sibling_tokens = [sibling_inputs] + [shift(piece, "c", 1) for piece in tokens[1:]]

    down_part, delta = small_terms(messages, inputs, x.reshape(1))
    down_part = [down_part, shift(down_part, "c", 1)]
    grad = gradient_pieces(messages, sibling_messages, numbers, tok)
    *down_part, _ = together(*down_part, grad[0])
    act = activation_pieces(tokens + sibling_tokens, down_part, row_offsets)

    grad_back, grad_far = travel(grad[3], "y", -1), travel(grad[2], "y", 1)
    act_back, act_far = travel(act[3], "z", -1), travel(act[2], "z", 1)
    grad_far, act_far = together(grad_far, act_far)
    grad_front = travel((grad[1].astype(f32) + grad_far.astype(f32)).astype(bf16), "y", 1)
    act_front = travel((act[1].astype(f32) + act_far.astype(f32)).astype(bf16), "z", 1)
    share, *_ = together(share, grad[0], act[0])
    shares = lax.all_to_all(share, "x", 0, 0)
    grad_front, grad_back, act_front, act_back, shares = together(grad_front, grad_back, act_front, act_back, shares)

    def total_of(*got):
        return sum(piece.astype(f32) for piece in got)

    def places(at):
        return [(at + ahead[k]) % ring for k in range(ring)]

    reduced = total_of(act[0], act_front, act_back)
    pieces = [cols(reduced, at * width, width) for at in places(x)]
    pieces = [pieces[0]] + [travel(pieces[k].astype(bf16), "x", k) for k in (1, 3, 2)]
    down_sum = total_of(*[piece[lane:] for piece in pieces]) / total
    act_factor = total_of(*[piece[:lane] for piece in pieces]) / total
    down_sum = down_sum + exchange(down_sum, "y", 1)
    down_sum = down_sum + exchange(down_sum, "y", 2)
    reduced = total_of(grad[0], grad_front, grad_back)
    extra = reduced[ring * lane :]
    pieces = [jnp.concatenate([rows(reduced, at * lane, lane), extra], 0) for at in places(z)]
    pieces = [pieces[0]] + [travel(pieces[k].astype(bf16), "z", k) for k in (1, 3, 2)]
    grad_factor = total_of(*[piece[:lane] for piece in pieces]) / total
    up_mean = total_of(*[piece[lane:] for piece in pieces]) * (adapter_scale / total)

    shares, _ = together(shares, pieces[1])
    input_gradient = (tn(delta, down) + jnp.sum(shares.astype(f32), 0)).astype(bf16)
    return input_gradient, act_factor, grad_factor, down_sum, up_mean


def solution(mesh):
    fine = Mesh(mesh.devices.reshape(ring, ring, 2, ring), ("y", "z", "c", "x"))
    dp = ("y", "z", "c")
    return jax.shard_map(
        per_device,
        mesh=fine,
        in_specs=(P(dp + ("x",), None), P(dp, "x"), P("x", None), P(), P(None, "x")),
        out_specs=(P(dp + ("x",), None), P(dp, "x"), P(dp, "x"), P(None, "x"), P(None, "x")),
        check_vma=False,
    )
```

```python
import functools

import jax
import jax.numpy as jnp
from jax import lax
from jax.experimental import pallas as pl
from jax.experimental.pallas import tpu as pltpu
from jax.sharding import Mesh, PartitionSpec as P

adapter_scale = 2.0
f32 = jnp.float32
bf16 = jnp.bfloat16
ring = 4
lane = 128
vmem = 60 * 2**20
hbm = pl.BlockSpec(memory_space=pltpu.MemorySpace.HBM)
light = pl.CostEstimate(flops=2**10, bytes_accessed=2**10, transcendentals=0)


def shift(array, axis, step):
    size = lax.axis_size(axis)
    return lax.ppermute(array, axis, [(i, (i + step) % size) for i in range(size)])


def exchange(array, axis, step):
    return lax.ppermute(array, axis, [(i, i ^ step) for i in range(lax.axis_size(axis))])


def travel(array, axis, step):
    size = lax.axis_size(axis)
    sign = (1, -1)
    order = ("c", axis) if axis == "x" else (axis, "c")
    place = (lambda i, c: size * c + i) if axis == "x" else (lambda i, c: 2 * i + c)
    pairs = [(place(i, c), place((i + step * sign[c]) % size, c)) for i in range(size) for c in range(2)]
    return lax.ppermute(array, order, pairs)


def together(*values):
    return lax.optimization_barrier(values)


def cols(array, start, width):
    return lax.dynamic_slice_in_dim(array, start, width, 1)


def rows(array, start, width):
    return lax.dynamic_slice_in_dim(array, start, width, 0)


def nt(left, right):
    return lax.dot_general(left, right, (((1,), (1,)), ((), ())), preferred_element_type=f32)


def tn(left, right):
    return lax.dot_general(left, right, (((0,), (0,)), ((), ())), preferred_element_type=f32)


def mm(left, right):
    return jnp.dot(left, right, preferred_element_type=f32)


def run_all(copies):
    for copy in copies:
        copy.start()
    for copy in copies:
        copy.wait()


def share_kernel(left, right, out):
    out[...] = mm(left[...], right[...]).astype(bf16)


def share_product(left, right, tile=512):
    return pl.pallas_call(
        share_kernel,
        grid=(right.shape[1] // tile,),
        in_specs=[
            pl.BlockSpec(left.shape, lambda j: (0, 0)),
            pl.BlockSpec((right.shape[0], tile), lambda j: (0, j)),
        ],
        out_specs=pl.BlockSpec((left.shape[0], tile), lambda j: (0, j)),
        out_shape=jax.ShapeDtypeStruct((left.shape[0], right.shape[1]), bf16),
        compiler_params=pltpu.CompilerParams(vmem_limit_bytes=vmem),
        cost_estimate=pl.CostEstimate(
            flops=2 * left.size * right.shape[1], bytes_accessed=2 * right.size, transcendentals=0
        ),
    )(left, right)


def small_kernel(place, *refs):
    messages, inputs, down, up = refs[:ring], refs[ring], refs[ring + 1], refs[ring + 2]
    held, weights, sems = refs[ring + 3 :]
    tok = inputs.shape[0]
    width = held.shape[2]
    rank = weights.shape[1]
    copies = []
    for k, ref in enumerate(messages):
        own = pl.ds(pl.multiple_of(place[0] * tok, tok), tok)
        copies.append(pltpu.make_async_copy(ref.at[own], held.at[k], sems.at[0, k]))
        copies.append(pltpu.make_async_copy(ref.at[pl.ds(ring * tok, rank)], weights.at[k], sems.at[1, k]))
    run_all(copies)
    both = [nt(weights[k], held[k]) for k in range(ring)]
    delta = (adapter_scale * ((both[0] + both[2]) + (both[1] + both[3]))).astype(bf16)
    up[...] = delta
    down[...] = mm(delta, inputs[...]).astype(bf16)


def small_terms(messages, inputs, place):
    tok, width = inputs.shape
    rank = 16
    return pl.pallas_call(
        small_kernel,
        grid_spec=pltpu.PrefetchScalarGridSpec(
            num_scalar_prefetch=1,
            grid=(1,),
            in_specs=[hbm] * ring + [pl.BlockSpec((tok, width), lambda j, o: (0, 0))],
            out_specs=[
                pl.BlockSpec((rank, width), lambda j, o: (0, 0)),
                pl.BlockSpec((rank, tok), lambda j, o: (0, 0)),
            ],
            scratch_shapes=[
                pltpu.VMEM((ring, tok, messages[0].shape[1]), bf16),
                pltpu.VMEM((ring, rank, messages[0].shape[1]), bf16),
                pltpu.SemaphoreType.DMA((2, ring)),
            ],
        ),
        out_shape=[jax.ShapeDtypeStruct((rank, width), bf16), jax.ShapeDtypeStruct((rank, tok), bf16)],
        compiler_params=pltpu.CompilerParams(vmem_limit_bytes=vmem),
        cost_estimate=light,
    )(place, *messages, inputs)


def stack(pairs, held, sems):
    copies = []
    at = 0
    for n, (ref, size) in enumerate(pairs):
        copies.append(pltpu.make_async_copy(ref.at[pl.ds(0, size)], held.at[pl.ds(at, size)], sems.at[n]))
        copies[-1].start()
        at += size
    return copies


def turn(held, offsets, turned):
    for i in range(ring):
        start = pl.multiple_of(offsets[i], lane)
        turned[i * lane : (i + 1) * lane] = held[:, pl.ds(start, lane)].T


def gradient_kernel(numbers, *refs):
    own, sibling, outs = refs[:ring], refs[ring : 2 * ring], refs[2 * ring : 3 * ring]
    held, low, turned, staged, sems, low_sems, out_sems = refs[3 * ring :]
    tok, width = held.shape[1] // 2, held.shape[2]
    sub = ring * lane
    rank = low.shape[0]
    offset = pl.multiple_of(numbers[3 * ring], lane)
    starts = (offset, tok - offset)
    arrivals, more = [], []
    for j in range(ring):
        for half, refs_of in enumerate((own, sibling)):
            part = pl.ds(pl.multiple_of(starts[half], lane), tok)
            arrivals.append(pltpu.make_async_copy(refs_of[j].at[pl.ds(0, tok)], held.at[j, part], sems.at[j, half]))
            arrivals[-1].start()
            start = pl.multiple_of(starts[half] + numbers[2 * ring + j], lane)
            more.append(
                pltpu.make_async_copy(
                    refs_of[j].at[pl.ds(tok + rank, rank), pl.ds(0, lane)],
                    low.at[:, pl.ds(start, lane)],
                    low_sems.at[half, j],
                )
            )
            more[-1].start()
    extra = None
    for j in range(ring):
        for copy in arrivals[2 * j : 2 * j + 2]:
            copy.wait()
        if j == 0:
            for copy in more:
                copy.wait()
            extra = mm(low[...], held[0]).astype(bf16)
            for k in range(ring):
                staged[k, sub:] = extra
        turn(held.at[j], numbers, turned)
        slot = numbers[ring + j]
        for i in range(2):
            part = slice(i * width // 2, (i + 1) * width // 2)
            staged[slot, :sub, part] = mm(turned[...], held[0, :, part]).astype(bf16)
        for k in range(ring):

            @pl.when(slot == k)
            def _():
                pltpu.make_async_copy(staged.at[k], outs[k], out_sems.at[k]).start()

    for k in range(ring):
        pltpu.make_async_copy(staged.at[k], outs[k], out_sems.at[k]).wait()


def gradient_pieces(own, sibling, numbers, tok):
    width = own[0].shape[1]
    sub = ring * lane
    rank = (own[0].shape[0] - tok) // 2
    return pl.pallas_call(
        gradient_kernel,
        grid_spec=pltpu.PrefetchScalarGridSpec(
            num_scalar_prefetch=1,
            grid=(1,),
            in_specs=[hbm] * (2 * ring),
            out_specs=[hbm] * ring,
            scratch_shapes=[
                pltpu.VMEM((ring, 2 * tok, width), bf16),
                pltpu.VMEM((rank, 2 * tok), bf16),
                pltpu.VMEM((sub, 2 * tok), bf16),
                pltpu.VMEM((ring, sub + rank, width), bf16),
                pltpu.SemaphoreType.DMA((ring, 2)),
                pltpu.SemaphoreType.DMA((2, ring)),
                pltpu.SemaphoreType.DMA((ring,)),
            ],
        ),
        out_shape=[jax.ShapeDtypeStruct((sub + rank, width), bf16)] * ring,
        compiler_params=pltpu.CompilerParams(vmem_limit_bytes=vmem),
        cost_estimate=light,
    )(numbers, *own, *sibling)


def activation_kernel(tile, numbers, *refs):
    count = len(refs) - ring - 8
    pieces, extra, outs = refs[:count], refs[count : count + 2], refs[count + 2 : count + 2 + ring]
    held, turned, staged, more, sems, out_sems = refs[count + 2 + ring :]
    width = held.shape[1]
    arrivals = stack([(ref, ref.shape[0]) for ref in pieces], held, sems)
    rest = [pltpu.make_async_copy(ref, more.at[i], sems.at[count + i]) for i, ref in enumerate(extra)]
    for copy in rest:
        copy.start()
    for copy in arrivals:
        copy.wait()
    turn(held, numbers, turned)
    for copy in rest:
        copy.wait()
    term = (more[0].astype(f32) + more[1].astype(f32)).astype(bf16)
    for k in range(ring):
        staged[k, lane:] = term
    sent = []
    for j in range(width // tile):
        part = slice(j * tile, (j + 1) * tile)
        result = mm(turned[...], held[:, part]).astype(bf16)
        for k in range(ring):
            staged[k, :lane, part] = result[k * lane : (k + 1) * lane]
            sent.append(pltpu.make_async_copy(staged.at[k, :, part], outs[k].at[:, part], out_sems.at[j, k]))
            sent[-1].start()
    for copy in sent:
        copy.wait()


def activation_pieces(pieces, extra, numbers, tile=512):
    count, width = len(pieces), pieces[0].shape[1]
    tokens = sum(piece.shape[0] for piece in pieces)
    rank = extra[0].shape[0]
    return pl.pallas_call(
        functools.partial(activation_kernel, tile),
        grid_spec=pltpu.PrefetchScalarGridSpec(
            num_scalar_prefetch=1,
            grid=(1,),
            in_specs=[hbm] * (count + 2),
            out_specs=[hbm] * ring,
            scratch_shapes=[
                pltpu.VMEM((tokens, width), bf16),
                pltpu.VMEM((ring * lane, tokens), bf16),
                pltpu.VMEM((ring, lane + rank, width), bf16),
                pltpu.VMEM((2, rank, width), bf16),
                pltpu.SemaphoreType.DMA((count + 2,)),
                pltpu.SemaphoreType.DMA((width // tile, ring)),
            ],
        ),
        out_shape=[jax.ShapeDtypeStruct((lane + rank, width), bf16)] * ring,
        compiler_params=pltpu.CompilerParams(vmem_limit_bytes=vmem),
        cost_estimate=light,
    )(numbers, *pieces, *extra)


def per_device(inputs, output_gradient, frozen, down, up):
    x, y, z, c = (lax.axis_index(name) for name in "xyzc")
    total = inputs.shape[0] * 128
    tok, width = output_gradient.shape
    own_rows = tok // ring
    rank = down.shape[0]
    steps = jnp.arange(ring, dtype=jnp.int32)
    sign = 1 - 2 * c
    ahead = sign * steps
    row_offsets = y * width + (z + ahead) % ring * (2 * lane) + c * lane
    slots = (jnp.where(c == 0, x - y, y - x) + steps) % ring
    numbers = jnp.concatenate([(2 * steps + c) * lane, slots, (x + ahead) % ring * lane, c[None] * tok])

    x_behind, x_ahead = travel(inputs, "y", 1), travel(inputs, "y", -1)
    low = jnp.pad(nt(down, inputs).astype(bf16), ((0, 0), (0, width - inputs.shape[0])))
    message = jnp.concatenate([output_gradient, up, low], 0)
    message_behind, message_ahead = travel(message, "x", 1), travel(message, "x", -1)
    sibling_message, sibling_inputs = shift(message, "c", 1), shift(inputs, "c", 1)
    share = share_product(output_gradient, frozen).reshape(ring, own_rows, -1)
    message_behind, message_ahead, x_behind, x_ahead, sibling_message, sibling_inputs, numbers, row_offsets = together(
        message_behind, message_ahead, x_behind, x_ahead, sibling_message, sibling_inputs, numbers, row_offsets
    )
    message_far = travel(message_behind, "x", 1)
    x_far = travel(x_behind, "y", 1)
    sibling_behind, sibling_ahead = shift(message_behind, "c", 1), shift(message_ahead, "c", 1)
    sibling_x_behind, sibling_x_ahead = shift(x_behind, "c", 1), shift(x_ahead, "c", 1)
    message_far, x_far, sibling_behind, sibling_ahead, sibling_x_behind, sibling_x_ahead, _ = together(
        message_far, x_far, sibling_behind, sibling_ahead, sibling_x_behind, sibling_x_ahead, share
    )
    messages = [message, message_ahead, message_far, message_behind]
    sibling_messages = [sibling_message, sibling_behind, shift(message_far, "c", 1), sibling_ahead]
    tokens = [inputs, x_ahead, x_behind, x_far]
    sibling_tokens = [sibling_inputs, sibling_x_ahead, sibling_x_behind, shift(x_far, "c", 1)]

    down_part, delta = small_terms(messages, inputs, x.reshape(1))
    down_part = [down_part, shift(down_part, "c", 1)]
    numbers, *down_part = together(numbers, *down_part)
    grad = gradient_pieces(messages, sibling_messages, numbers, tok)
    *down_part, _ = together(*down_part, grad[0])
    act = activation_pieces(tokens + sibling_tokens, down_part, row_offsets)

    shares = lax.all_to_all(share, "x", 0, 0)

    def pass_on(near, far, count):
        return jnp.concatenate([(near[:count].astype(f32) + far[:count].astype(f32)).astype(bf16), far[count:]], 0)

    grad_far, grad_back = travel(grad[2], "y", 1), travel(grad[3], "y", -1)
    act_far, act_back = travel(act[2], "z", 1), travel(act[3], "z", -1)
    grad_next = pass_on(grad[1], grad_far, ring * lane)
    grad_next, grad_back, act_far, act_back, shares = together(grad_next, grad_back, act_far, act_back, shares)
    grad_front = travel(grad_next, "y", 1)
    act_front = travel(pass_on(act[1], act_far, lane), "z", 1)
    input_gradient = (tn(delta, down) + jnp.sum(shares.astype(f32), 0)).astype(bf16)
    def total_of(own, far, front, back):
        return (own.astype(f32) + far.astype(f32)) + (front.astype(f32) + back.astype(f32))

    def sums_of(own, far, front, back, count):
        factor = own[:count].astype(f32) + (front[:count].astype(f32) + back[:count].astype(f32))
        return factor, total_of(own[count:], front[count:], far[count:], back[count:])

    def spread(pieces, axis):
        return pieces[0], *[travel(pieces[k], axis, k) for k in (2, 1, 3)]

    factor, term = sums_of(grad[0], grad_far, grad_front, grad_back, ring * lane)
    pieces = [
        jnp.concatenate([rows(factor, (z + sign * k + ring) % ring * lane, lane), term], 0).astype(bf16) for k in range(ring)
    ]
    input_gradient, act_front, *pieces = together(input_gradient, act_front, *pieces)
    pieces = spread(pieces, "z")
    grad_factor = total_of(*[piece[:lane] for piece in pieces]) / total
    up_mean = total_of(*[piece[lane:] for piece in pieces]) * (adapter_scale / total)
    factor, term = sums_of(act[0], act_far, act_front, act_back, lane)
    reduced = jnp.concatenate([factor, term], 0)
    pieces = [cols(reduced, (x + sign * k + ring) % ring * width, width).astype(bf16) for k in range(ring)]
    pieces = spread(pieces, "x")
    down_sum = total_of(*[piece[lane:] for piece in pieces]) / total
    act_factor = total_of(*[piece[:lane] for piece in pieces]) / total
    down_sum = total_of(*spread([down_sum] * ring, "y"))
    return input_gradient, act_factor, grad_factor, down_sum, up_mean


def solution(mesh):
    fine = Mesh(mesh.devices.reshape(ring, ring, 2, ring), ("y", "z", "c", "x"))
    dp = ("y", "z", "c")
    return jax.shard_map(
        per_device,
        mesh=fine,
        in_specs=(P(dp + ("x",), None), P(dp, "x"), P("x", None), P(), P(None, "x")),
        out_specs=(P(dp + ("x",), None), P(dp, "x"), P(dp, "x"), P(None, "x"), P(None, "x")),
        check_vma=False,
    )
```

```python
import functools

import jax
import jax.numpy as jnp
from jax import lax
from jax.experimental import pallas as pl
from jax.experimental.pallas import tpu as pltpu
from jax.sharding import Mesh, PartitionSpec as P

adapter_scale = 2.0
f32 = jnp.float32
bf16 = jnp.bfloat16
ring = 4
lane = 128
vmem = 60 * 2**20
hbm = pl.BlockSpec(memory_space=pltpu.MemorySpace.HBM)
light = pl.CostEstimate(flops=2**10, bytes_accessed=2**10, transcendentals=0)


def shift(array, axis, step):
    size = lax.axis_size(axis)
    return lax.ppermute(array, axis, [(i, (i + step) % size) for i in range(size)])


def exchange(array, axis, step):
    return lax.ppermute(array, axis, [(i, i ^ step) for i in range(lax.axis_size(axis))])


def travel(array, axis, step):
    size = lax.axis_size(axis)
    sign = (1, -1)
    order = ("c", axis) if axis == "x" else (axis, "c")
    place = (lambda i, c: size * c + i) if axis == "x" else (lambda i, c: 2 * i + c)
    pairs = [(place(i, c), place((i + step * sign[c]) % size, c)) for i in range(size) for c in range(2)]
    return lax.ppermute(array, order, pairs)


def together(*values):
    return lax.optimization_barrier(values)


def cols(array, start, width):
    return lax.dynamic_slice_in_dim(array, start, width, 1)


def rows(array, start, width):
    return lax.dynamic_slice_in_dim(array, start, width, 0)


def nt(left, right):
    return lax.dot_general(left, right, (((1,), (1,)), ((), ())), preferred_element_type=f32)


def tn(left, right):
    return lax.dot_general(left, right, (((0,), (0,)), ((), ())), preferred_element_type=f32)


def mm(left, right):
    return jnp.dot(left, right, preferred_element_type=f32)


def run_all(copies):
    for copy in copies:
        copy.start()
    for copy in copies:
        copy.wait()


def share_kernel(left, right, out):
    out[...] = mm(left[...], right[...]).astype(bf16)


def share_product(left, right, tile=1024):
    return pl.pallas_call(
        share_kernel,
        grid=(right.shape[1] // tile,),
        in_specs=[
            pl.BlockSpec(left.shape, lambda j: (0, 0)),
            pl.BlockSpec((right.shape[0], tile), lambda j: (0, j)),
        ],
        out_specs=pl.BlockSpec((left.shape[0], tile), lambda j: (0, j)),
        out_shape=jax.ShapeDtypeStruct((left.shape[0], right.shape[1]), bf16),
        compiler_params=pltpu.CompilerParams(vmem_limit_bytes=vmem),
        cost_estimate=pl.CostEstimate(
            flops=2 * left.size * right.shape[1], bytes_accessed=2 * right.size, transcendentals=0
        ),
    )(left, right)


def small_kernel(place, *refs):
    messages, inputs, down, up = refs[:ring], refs[ring], refs[ring + 1], refs[ring + 2]
    held, weights, sems = refs[ring + 3 :]
    tok = inputs.shape[0]
    width = held.shape[2]
    rank = weights.shape[1]
    copies = []
    for k, ref in enumerate(messages):
        own = pl.ds(pl.multiple_of(place[0] * tok, tok), tok)
        copies.append(pltpu.make_async_copy(ref.at[own], held.at[k], sems.at[0, k]))
        copies.append(pltpu.make_async_copy(ref.at[pl.ds(ring * tok, rank)], weights.at[k], sems.at[1, k]))
    run_all(copies)
    both = [nt(weights[k], held[k]) for k in range(ring)]
    delta = (adapter_scale * ((both[0] + both[2]) + (both[1] + both[3]))).astype(bf16)
    up[...] = delta
    down[...] = mm(delta, inputs[...]).astype(bf16)


def small_terms(messages, inputs, place):
    tok, width = inputs.shape
    rank = 16
    return pl.pallas_call(
        small_kernel,
        grid_spec=pltpu.PrefetchScalarGridSpec(
            num_scalar_prefetch=1,
            grid=(1,),
            in_specs=[hbm] * ring + [pl.BlockSpec((tok, width), lambda j, o: (0, 0))],
            out_specs=[
                pl.BlockSpec((rank, width), lambda j, o: (0, 0)),
                pl.BlockSpec((rank, tok), lambda j, o: (0, 0)),
            ],
            scratch_shapes=[
                pltpu.VMEM((ring, tok, messages[0].shape[1]), bf16),
                pltpu.VMEM((ring, rank, messages[0].shape[1]), bf16),
                pltpu.SemaphoreType.DMA((2, ring)),
            ],
        ),
        out_shape=[jax.ShapeDtypeStruct((rank, width), bf16), jax.ShapeDtypeStruct((rank, tok), bf16)],
        compiler_params=pltpu.CompilerParams(vmem_limit_bytes=vmem),
        cost_estimate=light,
    )(place, *messages, inputs)


def stack(pairs, held, sems):
    copies = []
    at = 0
    for n, (ref, size) in enumerate(pairs):
        copies.append(pltpu.make_async_copy(ref.at[pl.ds(0, size)], held.at[pl.ds(at, size)], sems.at[n]))
        copies[-1].start()
        at += size
    return copies


def turn(held, offsets, turned):
    for i in range(ring):
        start = pl.multiple_of(offsets[i], lane)
        turned[i * lane : (i + 1) * lane] = held[:, pl.ds(start, lane)].T


def gradient_kernel(numbers, *refs):
    own, sibling, outs = refs[:ring], refs[ring : 2 * ring], refs[2 * ring : 3 * ring]
    held, low, turned, staged, sems, low_sems, out_sems = refs[3 * ring :]
    tok, width = held.shape[1] // 2, held.shape[2]
    sub = ring * lane
    rank = low.shape[0]
    offset = pl.multiple_of(numbers[3 * ring], lane)
    starts = (offset, tok - offset)
    arrivals, more = [], []
    for j in range(ring):
        for half, refs_of in enumerate((own, sibling)):
            part = pl.ds(pl.multiple_of(starts[half], lane), tok)
            arrivals.append(pltpu.make_async_copy(refs_of[j].at[pl.ds(0, tok)], held.at[j, part], sems.at[j, half]))
            arrivals[-1].start()
            start = pl.multiple_of(starts[half] + numbers[2 * ring + j], lane)
            more.append(
                pltpu.make_async_copy(
                    refs_of[j].at[pl.ds(tok + rank, rank), pl.ds(0, lane)],
                    low.at[:, pl.ds(start, lane)],
                    low_sems.at[half, j],
                )
            )
            more[-1].start()
    extra = None
    for j in range(ring):
        for copy in arrivals[2 * j : 2 * j + 2]:
            copy.wait()
        if j == 0:
            for copy in more:
                copy.wait()
            extra = mm(low[...], held[0]).astype(bf16)
            for k in range(ring):
                staged[k, sub:] = extra
        turn(held.at[j], numbers, turned)
        slot = numbers[ring + j]
        for i in range(2):
            part = slice(i * width // 2, (i + 1) * width // 2)
            staged[slot, :sub, part] = mm(turned[...], held[0, :, part]).astype(bf16)
        for k in range(ring):

            @pl.when(slot == k)
            def _():
                pltpu.make_async_copy(staged.at[k], outs[k], out_sems.at[k]).start()

    for k in range(ring):
        pltpu.make_async_copy(staged.at[k], outs[k], out_sems.at[k]).wait()


def gradient_pieces(own, sibling, numbers, tok):
    width = own[0].shape[1]
    sub = ring * lane
    rank = (own[0].shape[0] - tok) // 2
    return pl.pallas_call(
        gradient_kernel,
        grid_spec=pltpu.PrefetchScalarGridSpec(
            num_scalar_prefetch=1,
            grid=(1,),
            in_specs=[hbm] * (2 * ring),
            out_specs=[hbm] * ring,
            scratch_shapes=[
                pltpu.VMEM((ring, 2 * tok, width), bf16),
                pltpu.VMEM((rank, 2 * tok), bf16),
                pltpu.VMEM((sub, 2 * tok), bf16),
                pltpu.VMEM((ring, sub + rank, width), bf16),
                pltpu.SemaphoreType.DMA((ring, 2)),
                pltpu.SemaphoreType.DMA((2, ring)),
                pltpu.SemaphoreType.DMA((ring,)),
            ],
        ),
        out_shape=[jax.ShapeDtypeStruct((sub + rank, width), bf16)] * ring,
        compiler_params=pltpu.CompilerParams(vmem_limit_bytes=vmem),
        cost_estimate=light,
    )(numbers, *own, *sibling)


def activation_kernel(tile, numbers, *refs):
    count = len(refs) - ring - 8
    pieces, extra, outs = refs[:count], refs[count : count + 2], refs[count + 2 : count + 2 + ring]
    held, turned, staged, more, sems, out_sems = refs[count + 2 + ring :]
    width = held.shape[1]
    arrivals = stack([(ref, ref.shape[0]) for ref in pieces], held, sems)
    rest = [pltpu.make_async_copy(ref, more.at[i], sems.at[count + i]) for i, ref in enumerate(extra)]
    for copy in rest:
        copy.start()
    for copy in arrivals:
        copy.wait()
    turn(held, numbers, turned)
    for copy in rest:
        copy.wait()
    term = (more[0].astype(f32) + more[1].astype(f32)).astype(bf16)
    for k in range(ring):
        staged[k, lane:] = term
    sent = []
    for j in range(width // tile):
        part = slice(j * tile, (j + 1) * tile)
        result = mm(turned[...], held[:, part]).astype(bf16)
        for k in range(ring):
            staged[k, :lane, part] = result[k * lane : (k + 1) * lane]
            sent.append(pltpu.make_async_copy(staged.at[k, :, part], outs[k].at[:, part], out_sems.at[j, k]))
            sent[-1].start()
    for copy in sent:
        copy.wait()


def activation_pieces(pieces, extra, numbers, tile=1024):
    count, width = len(pieces), pieces[0].shape[1]
    tokens = sum(piece.shape[0] for piece in pieces)
    rank = extra[0].shape[0]
    return pl.pallas_call(
        functools.partial(activation_kernel, tile),
        grid_spec=pltpu.PrefetchScalarGridSpec(
            num_scalar_prefetch=1,
            grid=(1,),
            in_specs=[hbm] * (count + 2),
            out_specs=[hbm] * ring,
            scratch_shapes=[
                pltpu.VMEM((tokens, width), bf16),
                pltpu.VMEM((ring * lane, tokens), bf16),
                pltpu.VMEM((ring, lane + rank, width), bf16),
                pltpu.VMEM((2, rank, width), bf16),
                pltpu.SemaphoreType.DMA((count + 2,)),
                pltpu.SemaphoreType.DMA((width // tile, ring)),
            ],
        ),
        out_shape=[jax.ShapeDtypeStruct((lane + rank, width), bf16)] * ring,
        compiler_params=pltpu.CompilerParams(vmem_limit_bytes=vmem),
        cost_estimate=light,
    )(numbers, *pieces, *extra)


def per_device(inputs, output_gradient, frozen, down, up):
    x, y, z, c = (lax.axis_index(name) for name in "xyzc")
    total = inputs.shape[0] * 128
    tok, width = output_gradient.shape
    own_rows = tok // ring
    rank = down.shape[0]
    steps = jnp.arange(ring, dtype=jnp.int32)
    sign = 1 - 2 * c
    ahead = sign * steps
    row_offsets = y * width + (z + ahead) % ring * (2 * lane) + c * lane
    slots = (jnp.where(c == 0, x - y, y - x) + steps) % ring
    numbers = jnp.concatenate([(2 * steps + c) * lane, slots, (x + ahead) % ring * lane, c[None] * tok])

    x_behind, x_ahead = travel(inputs, "y", 1), travel(inputs, "y", -1)
    low = jnp.pad(nt(down, inputs).astype(bf16), ((0, 0), (0, width - inputs.shape[0])))
    message = jnp.concatenate([output_gradient, up, low], 0)
    message_behind, message_ahead = travel(message, "x", 1), travel(message, "x", -1)
    sibling_message, sibling_inputs = shift(message, "c", 1), shift(inputs, "c", 1)
    share = share_product(output_gradient, frozen).reshape(ring, own_rows, -1)
    message_behind, message_ahead, x_behind, x_ahead, sibling_message, sibling_inputs, numbers, row_offsets = together(
        message_behind, message_ahead, x_behind, x_ahead, sibling_message, sibling_inputs, numbers, row_offsets
    )
    message_far = travel(message_behind, "x", 1)
    x_far = travel(x_behind, "y", 1)
    sibling_behind, sibling_ahead = shift(message_behind, "c", 1), shift(message_ahead, "c", 1)
    sibling_x_behind, sibling_x_ahead = shift(x_behind, "c", 1), shift(x_ahead, "c", 1)
    message_far, x_far, sibling_behind, sibling_ahead, sibling_x_behind, sibling_x_ahead, _ = together(
        message_far, x_far, sibling_behind, sibling_ahead, sibling_x_behind, sibling_x_ahead, share
    )
    messages = [message, message_ahead, message_far, message_behind]
    sibling_messages = [sibling_message, sibling_behind, shift(message_far, "c", 1), sibling_ahead]
    tokens = [inputs, x_ahead, x_behind, x_far]
    sibling_tokens = [sibling_inputs, sibling_x_ahead, sibling_x_behind, shift(x_far, "c", 1)]

    down_part, delta = small_terms(messages, inputs, x.reshape(1))
    down_part = [down_part, shift(down_part, "c", 1)]
    numbers, *down_part = together(numbers, *down_part)
    grad = gradient_pieces(messages, sibling_messages, numbers, tok)
    *down_part, _ = together(*down_part, grad[0])
    act = activation_pieces(tokens + sibling_tokens, down_part, row_offsets)

    shares = lax.all_to_all(share, "x", 0, 0)

    def pass_on(near, far, count):
        return jnp.concatenate([(near[:count].astype(f32) + far[:count].astype(f32)).astype(bf16), far[count:]], 0)

    grad_far, grad_back = travel(grad[2], "y", 1), travel(grad[3], "y", -1)
    act_far, act_back = travel(act[2], "z", 1), travel(act[3], "z", -1)
    grad_next = pass_on(grad[1], grad_far, ring * lane)
    grad_back, act_far, act_back, shares = together(grad_back, act_far, act_back, shares)
    grad_front = travel(grad_next, "y", 1)
    act_front = travel(pass_on(act[1], act_far, lane), "z", 1)
    input_gradient = (tn(delta, down) + jnp.sum(shares.astype(f32), 0)).astype(bf16)
    def total_of(own, far, front, back):
        return (own.astype(f32) + far.astype(f32)) + (front.astype(f32) + back.astype(f32))

    def sums_of(own, far, front, back, count):
        factor = own[:count].astype(f32) + (front[:count].astype(f32) + back[:count].astype(f32))
        return factor, total_of(own[count:], front[count:], far[count:], back[count:])

    def spread(pieces, axis):
        return pieces[0], *[travel(pieces[k], axis, k) for k in (2, 1, 3)]

    factor, term = sums_of(grad[0], grad_far, grad_front, grad_back, ring * lane)
    pieces = [
        jnp.concatenate([rows(factor, (z + sign * k + ring) % ring * lane, lane), term], 0).astype(bf16) for k in range(ring)
    ]
    input_gradient, act_front, *pieces = together(input_gradient, act_front, *pieces)
    pieces = spread(pieces, "z")
    grad_factor = total_of(*[piece[:lane] for piece in pieces]) / total
    up_mean = total_of(*[piece[lane:] for piece in pieces]) * (adapter_scale / total)
    factor, term = sums_of(act[0], act_far, act_front, act_back, lane)
    reduced = jnp.concatenate([factor, term], 0)
    pieces = [cols(reduced, (x + sign * k + ring) % ring * width, width).astype(bf16) for k in range(ring)]
    pieces = spread(pieces, "x")
    down_sum = total_of(*[piece[lane:] for piece in pieces]) / total
    act_factor = total_of(*[piece[:lane] for piece in pieces]) / total
    down_sum = total_of(*spread([down_sum] * ring, "y"))
    return input_gradient, act_factor, grad_factor, down_sum, up_mean


def solution(mesh):
    fine = Mesh(mesh.devices.reshape(ring, ring, 2, ring), ("y", "z", "c", "x"))
    dp = ("y", "z", "c")
    return jax.shard_map(
        per_device,
        mesh=fine,
        in_specs=(P(dp + ("x",), None), P(dp, "x"), P("x", None), P(), P(None, "x")),
        out_specs=(P(dp + ("x",), None), P(dp, "x"), P(dp, "x"), P(None, "x"), P(None, "x")),
        check_vma=False,
    )
```

```python
import functools

import jax
import jax.numpy as jnp
from jax import lax
from jax.experimental import pallas as pl
from jax.experimental.pallas import tpu as pltpu
from jax.sharding import Mesh, PartitionSpec as P

adapter_scale = 2.0
f32 = jnp.float32
bf16 = jnp.bfloat16
ring = 4
lane = 128
vmem = 60 * 2**20
hbm = pl.BlockSpec(memory_space=pltpu.MemorySpace.HBM)
light = pl.CostEstimate(flops=2**10, bytes_accessed=2**10, transcendentals=0)


def shift(array, axis, step):
    size = lax.axis_size(axis)
    return lax.ppermute(array, axis, [(i, (i + step) % size) for i in range(size)])


def exchange(array, axis, step):
    return lax.ppermute(array, axis, [(i, i ^ step) for i in range(lax.axis_size(axis))])


def travel(array, axis, step):
    size = lax.axis_size(axis)
    sign = (1, -1)
    order = ("c", axis) if axis == "x" else (axis, "c")
    place = (lambda i, c: size * c + i) if axis == "x" else (lambda i, c: 2 * i + c)
    pairs = [(place(i, c), place((i + step * sign[c]) % size, c)) for i in range(size) for c in range(2)]
    return lax.ppermute(array, order, pairs)


def together(*values):
    return lax.optimization_barrier(values)


def cols(array, start, width):
    return lax.dynamic_slice_in_dim(array, start, width, 1)


def rows(array, start, width):
    return lax.dynamic_slice_in_dim(array, start, width, 0)


def nt(left, right):
    return lax.dot_general(left, right, (((1,), (1,)), ((), ())), preferred_element_type=f32)


def tn(left, right):
    return lax.dot_general(left, right, (((0,), (0,)), ((), ())), preferred_element_type=f32)


def mm(left, right):
    return jnp.dot(left, right, preferred_element_type=f32)


def run_all(copies):
    for copy in copies:
        copy.start()
    for copy in copies:
        copy.wait()


def share_kernel(left, right, out):
    out[...] = mm(left[...], right[...]).astype(bf16)


def share_product(left, right, tile=1024):
    return pl.pallas_call(
        share_kernel,
        grid=(right.shape[1] // tile,),
        in_specs=[
            pl.BlockSpec(left.shape, lambda j: (0, 0)),
            pl.BlockSpec((right.shape[0], tile), lambda j: (0, j)),
        ],
        out_specs=pl.BlockSpec((left.shape[0], tile), lambda j: (0, j)),
        out_shape=jax.ShapeDtypeStruct((left.shape[0], right.shape[1]), bf16),
        compiler_params=pltpu.CompilerParams(vmem_limit_bytes=vmem),
        cost_estimate=pl.CostEstimate(
            flops=2 * left.size * right.shape[1], bytes_accessed=2 * right.size, transcendentals=0
        ),
    )(left, right)


def small_kernel(place, *refs):
    messages, inputs, down, up = refs[:ring], refs[ring], refs[ring + 1], refs[ring + 2]
    held, weights, sems = refs[ring + 3 :]
    tok = inputs.shape[0]
    width = held.shape[2]
    rank = weights.shape[1]
    copies = []
    for k, ref in enumerate(messages):
        own = pl.ds(pl.multiple_of(place[0] * tok, tok), tok)
        copies.append(pltpu.make_async_copy(ref.at[own], held.at[k], sems.at[0, k]))
        copies.append(pltpu.make_async_copy(ref.at[pl.ds(ring * tok, rank)], weights.at[k], sems.at[1, k]))
    run_all(copies)
    both = [nt(weights[k], held[k]) for k in range(ring)]
    delta = (adapter_scale * ((both[0] + both[2]) + (both[1] + both[3]))).astype(bf16)
    up[...] = delta
    down[...] = mm(delta, inputs[...]).astype(bf16)


def small_terms(messages, inputs, place):
    tok, width = inputs.shape
    rank = 16
    return pl.pallas_call(
        small_kernel,
        grid_spec=pltpu.PrefetchScalarGridSpec(
            num_scalar_prefetch=1,
            grid=(1,),
            in_specs=[hbm] * ring + [pl.BlockSpec((tok, width), lambda j, o: (0, 0))],
            out_specs=[
                pl.BlockSpec((rank, width), lambda j, o: (0, 0)),
                pl.BlockSpec((rank, tok), lambda j, o: (0, 0)),
            ],
            scratch_shapes=[
                pltpu.VMEM((ring, tok, messages[0].shape[1]), bf16),
                pltpu.VMEM((ring, rank, messages[0].shape[1]), bf16),
                pltpu.SemaphoreType.DMA((2, ring)),
            ],
        ),
        out_shape=[jax.ShapeDtypeStruct((rank, width), bf16), jax.ShapeDtypeStruct((rank, tok), bf16)],
        compiler_params=pltpu.CompilerParams(vmem_limit_bytes=vmem),
        cost_estimate=light,
    )(place, *messages, inputs)


def stack(pairs, held, sems):
    copies = []
    at = 0
    for n, (ref, size) in enumerate(pairs):
        copies.append(pltpu.make_async_copy(ref.at[pl.ds(0, size)], held.at[pl.ds(at, size)], sems.at[n]))
        copies[-1].start()
        at += size
    return copies


def turn(held, offsets, turned):
    for i in range(ring):
        start = pl.multiple_of(offsets[i], lane)
        turned[i * lane : (i + 1) * lane] = held[:, pl.ds(start, lane)].T


def gradient_kernel(numbers, *refs):
    own, sibling, outs = refs[:ring], refs[ring : 2 * ring], refs[2 * ring : 3 * ring]
    held, low, turned, staged, sems, low_sems, out_sems = refs[3 * ring :]
    tok, width = held.shape[1] // 2, held.shape[2]
    sub = ring * lane
    rank = low.shape[0]
    offset = pl.multiple_of(numbers[3 * ring], lane)
    starts = (offset, tok - offset)
    arrivals, more = [], []
    for j in range(ring):
        for half, refs_of in enumerate((own, sibling)):
            part = pl.ds(pl.multiple_of(starts[half], lane), tok)
            arrivals.append(pltpu.make_async_copy(refs_of[j].at[pl.ds(0, tok)], held.at[j, part], sems.at[j, half]))
            arrivals[-1].start()
            start = pl.multiple_of(starts[half] + numbers[2 * ring + j], lane)
            more.append(
                pltpu.make_async_copy(
                    refs_of[j].at[pl.ds(tok + rank, rank), pl.ds(0, lane)],
                    low.at[:, pl.ds(start, lane)],
                    low_sems.at[half, j],
                )
            )
            more[-1].start()
    extra = None
    for j in range(ring):
        for copy in arrivals[2 * j : 2 * j + 2]:
            copy.wait()
        if j == 0:
            for copy in more:
                copy.wait()
            extra = mm(low[...], held[0]).astype(bf16)
            for k in range(ring):
                staged[k, sub:] = extra
        turn(held.at[j], numbers, turned)
        slot = numbers[ring + j]
        for i in range(2):
            part = slice(i * width // 2, (i + 1) * width // 2)
            staged[slot, :sub, part] = mm(turned[...], held[0, :, part]).astype(bf16)
        for k in range(ring):

            @pl.when(slot == k)
            def _():
                pltpu.make_async_copy(staged.at[k], outs[k], out_sems.at[k]).start()

    for k in range(ring):
        pltpu.make_async_copy(staged.at[k], outs[k], out_sems.at[k]).wait()


def gradient_pieces(own, sibling, numbers, tok):
    width = own[0].shape[1]
    sub = ring * lane
    rank = (own[0].shape[0] - tok) // 2
    return pl.pallas_call(
        gradient_kernel,
        grid_spec=pltpu.PrefetchScalarGridSpec(
            num_scalar_prefetch=1,
            grid=(1,),
            in_specs=[hbm] * (2 * ring),
            out_specs=[hbm] * ring,
            scratch_shapes=[
                pltpu.VMEM((ring, 2 * tok, width), bf16),
                pltpu.VMEM((rank, 2 * tok), bf16),
                pltpu.VMEM((sub, 2 * tok), bf16),
                pltpu.VMEM((ring, sub + rank, width), bf16),
                pltpu.SemaphoreType.DMA((ring, 2)),
                pltpu.SemaphoreType.DMA((2, ring)),
                pltpu.SemaphoreType.DMA((ring,)),
            ],
        ),
        out_shape=[jax.ShapeDtypeStruct((sub + rank, width), bf16)] * ring,
        compiler_params=pltpu.CompilerParams(vmem_limit_bytes=vmem),
        cost_estimate=light,
    )(numbers, *own, *sibling)


def activation_kernel(tile, numbers, *refs):
    count = len(refs) - ring - 8
    pieces, extra, outs = refs[:count], refs[count : count + 2], refs[count + 2 : count + 2 + ring]
    held, turned, staged, more, sems, out_sems = refs[count + 2 + ring :]
    width = held.shape[1]
    arrivals = stack([(ref, ref.shape[0]) for ref in pieces], held, sems)
    rest = [pltpu.make_async_copy(ref, more.at[i], sems.at[count + i]) for i, ref in enumerate(extra)]
    for copy in rest:
        copy.start()
    for copy in arrivals:
        copy.wait()
    turn(held, numbers, turned)
    for copy in rest:
        copy.wait()
    term = (more[0].astype(f32) + more[1].astype(f32)).astype(bf16)
    for k in range(ring):
        staged[k, lane:] = term
    sent = []
    for j in range(width // tile):
        part = slice(j * tile, (j + 1) * tile)
        result = mm(turned[...], held[:, part]).astype(bf16)
        for k in range(ring):
            staged[k, :lane, part] = result[k * lane : (k + 1) * lane]
            sent.append(pltpu.make_async_copy(staged.at[k, :, part], outs[k].at[:, part], out_sems.at[j, k]))
            sent[-1].start()
    for copy in sent:
        copy.wait()


def activation_pieces(pieces, extra, numbers, tile=1024):
    count, width = len(pieces), pieces[0].shape[1]
    tokens = sum(piece.shape[0] for piece in pieces)
    rank = extra[0].shape[0]
    return pl.pallas_call(
        functools.partial(activation_kernel, tile),
        grid_spec=pltpu.PrefetchScalarGridSpec(
            num_scalar_prefetch=1,
            grid=(1,),
            in_specs=[hbm] * (count + 2),
            out_specs=[hbm] * ring,
            scratch_shapes=[
                pltpu.VMEM((tokens, width), bf16),
                pltpu.VMEM((ring * lane, tokens), bf16),
                pltpu.VMEM((ring, lane + rank, width), bf16),
                pltpu.VMEM((2, rank, width), bf16),
                pltpu.SemaphoreType.DMA((count + 2,)),
                pltpu.SemaphoreType.DMA((width // tile, ring)),
            ],
        ),
        out_shape=[jax.ShapeDtypeStruct((lane + rank, width), bf16)] * ring,
        compiler_params=pltpu.CompilerParams(vmem_limit_bytes=vmem),
        cost_estimate=light,
    )(numbers, *pieces, *extra)


def per_device(inputs, output_gradient, frozen, down, up):
    x, y, z, c = (lax.axis_index(name) for name in "xyzc")
    total = inputs.shape[0] * 128
    tok, width = output_gradient.shape
    own_rows = tok // ring
    rank = down.shape[0]
    steps = jnp.arange(ring, dtype=jnp.int32)
    sign = 1 - 2 * c
    ahead = sign * steps
    row_offsets = y * width + (z + ahead) % ring * (2 * lane) + c * lane
    slots = (jnp.where(c == 0, x - y, y - x) + steps) % ring
    numbers = jnp.concatenate([(2 * steps + c) * lane, slots, (x + ahead) % ring * lane, c[None] * tok])

    x_behind, x_ahead = travel(inputs, "y", 1), travel(inputs, "y", -1)
    low = jnp.pad(nt(down, inputs).astype(bf16), ((0, 0), (0, width - inputs.shape[0])))
    message = jnp.concatenate([output_gradient, up, low], 0)
    message_behind, message_ahead = travel(message, "x", 1), travel(message, "x", -1)
    sibling_message, sibling_inputs = shift(message, "c", 1), shift(inputs, "c", 1)
    share = share_product(output_gradient, frozen).reshape(ring, own_rows, -1)
    message_behind, message_ahead, x_behind, x_ahead, sibling_message, sibling_inputs, numbers, row_offsets = together(
        message_behind, message_ahead, x_behind, x_ahead, sibling_message, sibling_inputs, numbers, row_offsets
    )
    message_far = travel(message_behind, "x", 1)
    x_far = travel(x_behind, "y", 1)
    sibling_behind, sibling_ahead = shift(message_behind, "c", 1), shift(message_ahead, "c", 1)
    sibling_x_behind, sibling_x_ahead = shift(x_behind, "c", 1), shift(x_ahead, "c", 1)
    message_far, x_far, sibling_behind, sibling_ahead, sibling_x_behind, sibling_x_ahead, _ = together(
        message_far, x_far, sibling_behind, sibling_ahead, sibling_x_behind, sibling_x_ahead, share
    )
    messages = [message, message_ahead, message_far, message_behind]
    sibling_messages = [sibling_message, sibling_behind, shift(message_far, "c", 1), sibling_ahead]
    tokens = [inputs, x_ahead, x_behind, x_far]
    sibling_tokens = [sibling_inputs, sibling_x_ahead, sibling_x_behind, shift(x_far, "c", 1)]

    down_part, delta = small_terms(messages, inputs, x.reshape(1))
    down_part = [down_part, shift(down_part, "c", 1)]
    numbers, *down_part = together(numbers, *down_part)
    grad = gradient_pieces(messages, sibling_messages, numbers, tok)
    *down_part, _ = together(*down_part, grad[0])
    act = activation_pieces(tokens + sibling_tokens, down_part, row_offsets)

    shares = lax.all_to_all(share, "x", 0, 0)

    def pass_on(near, far, count):
        return jnp.concatenate([(near[:count].astype(f32) + far[:count].astype(f32)).astype(bf16), far[count:]], 0)

    grad_far, grad_back = travel(grad[2], "y", 1), travel(grad[3], "y", -1)
    act_far, act_back = travel(act[2], "z", 1), travel(act[3], "z", -1)
    grad_next = pass_on(grad[1], grad_far, ring * lane)
    act_far, act_back, shares = together(act_far, act_back, shares)
    grad_front = travel(grad_next, "y", 1)
    act_front = travel(pass_on(act[1], act_far, lane), "z", 1)
    input_gradient = (tn(delta, down) + jnp.sum(shares.astype(f32), 0)).astype(bf16)
    def total_of(own, far, front, back):
        return (own.astype(f32) + far.astype(f32)) + (front.astype(f32) + back.astype(f32))

    def sums_of(own, far, front, back, count):
        factor = own[:count].astype(f32) + (front[:count].astype(f32) + back[:count].astype(f32))
        return factor, total_of(own[count:], front[count:], far[count:], back[count:])

    def spread(pieces, axis):
        return pieces[0], *[travel(pieces[k], axis, k) for k in (2, 1, 3)]

    factor, term = sums_of(grad[0], grad_far, grad_front, grad_back, ring * lane)
    pieces = [
        jnp.concatenate([rows(factor, (z + sign * k + ring) % ring * lane, lane), term], 0).astype(bf16) for k in range(ring)
    ]
    input_gradient, act_front, *pieces = together(input_gradient, act_front, *pieces)
    pieces = spread(pieces, "z")
    grad_factor = total_of(*[piece[:lane] for piece in pieces]) / total
    up_mean = total_of(*[piece[lane:] for piece in pieces]) * (adapter_scale / total)
    factor, term = sums_of(act[0], act_far, act_front, act_back, lane)
    reduced = jnp.concatenate([factor, term], 0)
    pieces = [cols(reduced, (x + sign * k + ring) % ring * width, width).astype(bf16) for k in range(ring)]
    pieces = spread(pieces, "x")
    down_sum = total_of(*[piece[lane:] for piece in pieces]) / total
    act_factor = total_of(*[piece[:lane] for piece in pieces]) / total
    down_sum = total_of(*spread([down_sum] * ring, "y"))
    return input_gradient, act_factor, grad_factor, down_sum, up_mean


def solution(mesh):
    fine = Mesh(mesh.devices.reshape(ring, ring, 2, ring), ("y", "z", "c", "x"))
    dp = ("y", "z", "c")
    return jax.shard_map(
        per_device,
        mesh=fine,
        in_specs=(P(dp + ("x",), None), P(dp, "x"), P("x", None), P(), P(None, "x")),
        out_specs=(P(dp + ("x",), None), P(dp, "x"), P(dp, "x"), P(None, "x"), P(None, "x")),
        check_vma=False,
    )
```
